1024 devices in a mesh: gx: 16 (over z, core), gy: 64 (over x, y).
Axes of the slice: x: 8, y: 8, z: 8, core: 2. Of those that a mesh axis runs over, the one named last changes fastest.
Arguments:
- tokens: bfloat16 [512, 10240], P('gy', 'gx'), may hold values from -6 to 6
- gate_pre: bfloat16 [512, 40960], P('gx', 'gy'), may hold values from -6 to 6
- up_pre: bfloat16 [512, 40960], P('gx', 'gy'), may hold values from -6 to 6
- hidden_grad: bfloat16 [512, 40960], P('gx', 'gy'), may hold values from -5 to 5
- w_gate: bfloat16 [10240, 40960], P('gx', 'gy'), may hold values from -0.0625 to 0.0625
- w_up: bfloat16 [10240, 40960], P('gx', 'gy'), may hold values from -0.0625 to 0.0625
Outputs:
- input_grad: bfloat16 [512, 10240], P('gy', 'gx')
- gate_weight_grad: bfloat16 [10240, 40960], P('gx', 'gy')
- up_weight_grad: bfloat16 [10240, 40960], P('gx', 'gy')
The draws below stay inside these ranges and needn't reach their ends.
All inputs are finite; a program needn't handle non-finite values.
Results may differ from the reference program's by a relative error of at most 0.0049.
Values may be sent and summed in bfloat16 or wider, within the bound.
A program may use at most 32 MiB of HBM per device.

```python
import jax
import jax.numpy as jnp
from jax import lax

D = 10240
FF = 40960
TOKENS = 512


def level_of(key, extent, shards, smallest, largest):
    def one(axis_at, shards_of):
        steps = jax.random.uniform(jax.random.fold_in(jax.random.fold_in(key, 6), axis_at), (shards_of,), jnp.float32, smallest / len(shards), largest / len(shards))
        return jnp.repeat(jnp.exp(steps), extent[axis_at] // shards_of).reshape((-1,) + (1,) * (len(extent) - axis_at - 1))

    loudness = one(*shards[0])
    for cut in shards[1:]:
        loudness = loudness * one(*cut)
    return loudness


def normal_values(stream_key, extent, scale, most, shards=(), kind=jnp.bfloat16):
    level = level_of(stream_key, extent, shards, -0.22, 0.18) if shards else 1.0
    array = jax.random.normal(stream_key, extent, jnp.float32) * scale * level
    return jnp.minimum(jnp.maximum(array, -most), most).astype(kind)


def setup_inputs(seed: int = 0) -> dict:
    streams_of = jax.random.split(jax.random.key(seed), 7)
    return {
        "tokens": normal_values(streams_of[0], (TOKENS, D), 1.0, 6.0, ((0, 64), (1, 16))),
        "gate_pre": normal_values(streams_of[1], (TOKENS, FF), 1.0, 6.0, ((0, 16), (1, 64))),
        "up_pre": normal_values(streams_of[2], (TOKENS, FF), 1.0, 6.0, ((0, 16), (1, 64))),
        "hidden_grad": normal_values(streams_of[3], (TOKENS, FF), 0.35, 5.0, ((0, 16), (1, 64))),
        "w_gate": normal_values(streams_of[4], (D, FF), D ** -0.5, 0.0625, ((0, 16), (1, 64))),
        "w_up": normal_values(streams_of[5], (D, FF), D ** -0.5, 0.0625, ((0, 16), (1, 64))),
    }


def contract_last(left, right):
    return lax.dot_general(left, right, (((1,), (1,)), ((), ())), preferred_element_type=jnp.float32)


def contract_first(left, right):
    return lax.dot_general(left, right, (((0,), (0,)), ((), ())), preferred_element_type=jnp.float32)


def reference(tokens, gate_pre, up_pre, hidden_grad, w_gate, w_up):
    gate_vals = gate_pre.astype(jnp.float32)
    up_vals = up_pre.astype(jnp.float32)
    grad_vals = hidden_grad.astype(jnp.float32)
    sig = jax.nn.sigmoid(gate_vals)
    gate_grad = (grad_vals * up_vals * sig * (1.0 + gate_vals * (1.0 - sig))).astype(jnp.bfloat16)
    up_grad = (grad_vals * gate_vals * sig).astype(jnp.bfloat16)
    input_grad = (contract_last(gate_grad, w_gate) + contract_last(up_grad, w_up)).astype(jnp.bfloat16)
    gate_weight_grad = contract_first(tokens, gate_grad).astype(jnp.bfloat16)
    up_weight_grad = contract_first(tokens, up_grad).astype(jnp.bfloat16)
    return input_grad, gate_weight_grad, up_weight_grad
```

```python
import functools

import jax
import jax.numpy as jnp
from jax import lax
from jax.experimental import pallas as pl
from jax.experimental.pallas import tpu as pltpu
from jax.sharding import PartitionSpec as P

MESH = pl.DeviceIdType.MESH
F32 = jnp.float32
BF16 = jnp.bfloat16


def slot_of(delta, n):
    if delta == 0:
        return 0
    if delta <= n // 2 - 1:
        return 2 * delta - 1
    if delta == n // 2:
        return n - 1
    return 2 * (n - delta)


def slot_dynamic(delta, n):
    near = jnp.where(delta == n // 2, n - 1, 2 * delta - 1)
    far = 2 * (n - delta)
    return jnp.where(delta == 0, 0, jnp.where(delta <= n // 2, near, far))


def delta_of(slot, n):
    return next(d for d in range(n) if slot_of(d, n) == slot)


def groups_of(n):
    groups = [(0, 3)]
    for step in range(2, n // 2):
        groups.append((2 * step - 1, 2 * step + 1))
    groups.append((n - 1, n))
    return groups


def kernel(n, rows, *refs):
    (
        tok_hbm, gate_hbm, up_hbm, grad_hbm, wg_hbm, wu_hbm,
        out_ref, dwg_hbm, dwu_hbm,
        gate_v, up_v, grad_v, wg, wu, gu, tok, tok2, dwg, dwu, sums, part2,
        *more,
    ) = refs
    groups = groups_of(n)
    ng = len(groups)
    parts = more[:ng]
    recvs = more[ng:2 * ng]
    (
        load_sem, store_sem, z_send, z_recv, sib_send, sib_recv,
        t1_send, t1_recv, t2_send, t2_recv, s1_send, s1_recv, s2_send, s2_recv,
    ) = more[2 * ng:]
    half = n // 2
    gx = lax.axis_index("gx")
    gy = lax.axis_index("gy")
    z, c = gx // 2, gx % 2
    x, y = gy // n, gy % n
    first = c == 0
    a = jnp.where(first, x, y)
    b = jnp.where(first, y, x)

    def at_ab(a_at, b_at):
        return (gx, jnp.where(first, a_at * n + b_at, b_at * n + a_at))

    def at_z(z_at):
        return (z_at * 2 + c, gy)

    sibling = (gx + 1 - 2 * c, gy)
    up_z = at_z((z + 1) % n)
    down_z = at_z((z + n - 1) % n)
    next_a = at_ab((a + 1) % n, b)
    prev_a = at_ab((a + n - 1) % n, b)

    def remote(src, dst, send, recv, to):
        copy = pltpu.make_async_remote_copy(
            src_ref=src, dst_ref=dst, send_sem=send, recv_sem=recv,
            device_id=to, device_id_type=MESH,
        )
        copy.start()
        return copy

    loads = [
        pltpu.make_async_copy(src, dst, load_sem.at[i])
        for i, (src, dst) in enumerate(
            (
                (gate_hbm, gate_v), (up_hbm, up_v), (grad_hbm, grad_v),
                (tok_hbm, tok.at[a, b]),
                (wg_hbm, wg), (wu_hbm, wu),
            )
        )
    ]
    for load in loads:
        load.start()

    barrier = pltpu.get_barrier_semaphore()

    def greet(to):
        pl.semaphore_signal(barrier, inc=1, device_id=to, device_id_type=MESH)

    greet(sibling)
    greet(up_z)
    greet(down_z)
    greet(next_a)
    greet(prev_a)
    for k in range(1, n):
        greet(at_ab(a, (b + k) % n))
    for j in range(n):
        @pl.when(jnp.logical_not((a == j) & (b == y)))
        def _():
            greet(at_ab(j, y))

    for load in loads[:3]:
        load.wait()
    gate = gate_v[...].astype(F32)
    up = up_v[...].astype(F32)
    grad = grad_v[...].astype(F32)
    sig = 1.0 / (1.0 + jnp.exp(-gate))
    gu[0, 0, c] = (grad * up * sig * (1.0 + gate * (1.0 - sig))).astype(BF16)
    gu[1, 0, c] = (grad * gate * sig).astype(BF16)

    self_dest = jnp.where(b == y, 1, 0)
    pl.semaphore_wait(barrier, 5 + (n - 1) + n - self_dest)

    pending = []

    def ring_slot(direction, step):
        return slot_of((n - step) % n if direction == 0 else step, n)

    def ring_send(direction, step, chunk):
        pending.append(
            remote(
                gu.at[chunk, ring_slot(direction, step - 1), c],
                gu.at[chunk, ring_slot(direction, step), c],
                z_send.at[direction, step - 1, chunk],
                z_recv.at[direction, step - 1, chunk],
                up_z if direction == 0 else down_z,
            )
        )

    def ring_wait(direction, step, chunk):
        slot = ring_slot(direction, step)
        pltpu.make_async_remote_copy(
            src_ref=gu.at[chunk, slot, c], dst_ref=gu.at[chunk, slot, c],
            send_sem=z_send.at[direction, step - 1, chunk],
            recv_sem=z_recv.at[direction, step - 1, chunk],
            device_id=sibling, device_id_type=MESH,
        ).wait_recv()

    def travels(direction, step, chunk):
        return step < half or (step == half and chunk == direction)

    def sib_share(slot, chunk):
        pending.append(
            remote(
                gu.at[chunk, slot, c], gu.at[chunk, slot, c],
                sib_send.at[slot, chunk], sib_recv.at[slot, chunk], sibling,
            )
        )

    def sib_wait(slot, chunk):
        pltpu.make_async_remote_copy(
            src_ref=gu.at[chunk, slot, 1 - c], dst_ref=gu.at[chunk, slot, 1 - c],
            send_sem=sib_send.at[slot, chunk], recv_sem=sib_recv.at[slot, chunk],
            device_id=sibling, device_id_type=MESH,
        ).wait_recv()

    for chunk in range(2):
        for direction in range(2):
            ring_send(direction, 1, chunk)
    for chunk in range(2):
        sib_share(0, chunk)

    loads[3].wait()
    for k in range(1, n):
        pending.append(
            remote(
                tok.at[a, b], tok.at[a, b], t1_send.at[k - 1], t1_recv.at[k - 1],
                at_ab(a, (b + k) % n),
            )
        )

    def tok_send(direction, step):
        block = (a - (step - 1) + n) % n if direction == 0 else (a + step - 1) % n
        lo, hi = tok_part(direction, step)
        pending.append(
            remote(
                tok.at[block, lo:hi], tok.at[block, lo:hi],
                t2_send.at[direction, step - 1], t2_recv.at[direction, step - 1],
                next_a if direction == 0 else prev_a,
            )
        )

    def tok_part(direction, step):
        if step < half:
            return 0, n
        return (0, half) if direction == 0 else (half, n)

    def tok_wait(direction, step):
        block = (a - step + n) % n if direction == 0 else (a + step) % n
        lo, hi = tok_part(direction, step)
        pltpu.make_async_remote_copy(
            src_ref=tok.at[block, lo:hi], dst_ref=tok.at[block, lo:hi],
            send_sem=t2_send.at[direction, step - 1],
            recv_sem=t2_recv.at[direction, step - 1],
            device_id=sibling, device_id_type=MESH,
        ).wait_recv()

    def tok_first():
        for k in range(1, n):
            pltpu.make_async_remote_copy(
                src_ref=tok.at[a, b], dst_ref=tok.at[a, (b + n - k) % n],
                send_sem=t1_send.at[k - 1], recv_sem=t1_recv.at[k - 1],
                device_id=sibling, device_id_type=MESH,
            ).wait_recv()
        for direction in range(2):
            tok_send(direction, 1)

    def multiply(index):
        lo, hi = groups[index]
        m = (hi - lo) * 2 * rows
        left_g = gu[0, lo:hi].reshape(m, gu.shape[-1])
        left_u = gu[1, lo:hi].reshape(m, gu.shape[-1])
        dims = (((1,), (1,)), ((), ()))
        total = lax.dot_general(left_g, wg[...], dims, preferred_element_type=F32)
        total += lax.dot_general(left_u, wu[...], dims, preferred_element_type=F32)
        per = 2 * rows // n
        for i in range(hi - lo):
            parts[index][:, i] = (
                total[i * 2 * rows:(i + 1) * 2 * rows]
                .reshape(n, per, total.shape[-1]).astype(BF16)
            )
        for k in range(1, n):
            to = (b + k) % n
            pending.append(
                remote(
                    parts[index].at[to], recvs[index].at[k - 1],
                    s1_send.at[index, k - 1], s1_recv.at[index, k - 1], at_ab(a, to),
                )
            )

    def reduce_first(index):
        lo, hi = groups[index]
        for k in range(1, n):
            pltpu.make_async_remote_copy(
                src_ref=recvs[index].at[k - 1], dst_ref=recvs[index].at[k - 1],
                send_sem=s1_send.at[index, k - 1], recv_sem=s1_recv.at[index, k - 1],
                device_id=sibling, device_id_type=MESH,
            ).wait_recv()
        total = parts[index][b].astype(F32)
        for k in range(1, n):
            total += recvs[index][k - 1].astype(F32)
        sums[lo:hi] = total.astype(BF16)
        for slot in range(lo, hi):
            owner_x = (z + delta_of(slot, n)) % n
            mine = (owner_x == x) & (b == y)

            @pl.when(mine)
            def _():
                pltpu.make_async_copy(
                    sums.at[slot], part2.at[a], s2_recv.at[a]
                ).start()

            @pl.when(jnp.logical_not(mine))
            def _():
                remote(
                    sums.at[slot], part2.at[a], s2_send.at[slot], s2_recv.at[a],
                    (gx, owner_x * n + b),
                )

    def reduce_sent(slot):
        owner_x = (z + delta_of(slot, n)) % n
        mine = (owner_x == x) & (b == y)

        @pl.when(jnp.logical_not(mine))
        def _():
            pltpu.make_async_remote_copy(
                src_ref=sums.at[slot], dst_ref=part2.at[a],
                send_sem=s2_send.at[slot], recv_sem=s2_recv.at[a],
                device_id=sibling, device_id_type=MESH,
            ).wait_send()

    def weights(chunk, result, to, sem):
        right = gu[chunk].reshape(n * 2 * rows, gu.shape[-1])
        result[...] = lax.dot_general(
            tok2[...], right, (((0,), (0,)), ((), ())), preferred_element_type=F32
        ).astype(BF16)
        store = pltpu.make_async_copy(result, to, sem)
        store.start()
        return store

    tok_first()
    for step in range(1, half + 1):
        for chunk in range(2):
            for direction in range(2):
                if not travels(direction, step, chunk):
                    continue
                ring_wait(direction, step, chunk)
                if travels(direction, step + 1, chunk):
                    ring_send(direction, step + 1, chunk)
                sib_share(ring_slot(direction, step), chunk)
        for direction in range(2):
            tok_wait(direction, step)
            if step < half:
                tok_send(direction, step + 1)
        if step == 1:
            for chunk in range(2):
                sib_wait(0, chunk)
            loads[4].wait()
            loads[5].wait()
        for chunk in range(2):
            for slot in sorted({ring_slot(0, step), ring_slot(1, step)}):
                sib_wait(slot, chunk)
        multiply(step - 1)
        if step >= 2:
            reduce_first(step - 2)

    for slot in range(n):
        block = (z + delta_of(slot, n)) % n
        for pair in range(n // 2):
            two = []
            for at in (2 * pair, 2 * pair + 1):
                i = jnp.where(first, block, at)
                j = jnp.where(first, at, block)
                two.append(tok[i, j].astype(F32))
            per = tok.shape[2]
            start = (slot * n + 2 * pair) * per
            tok2[start:start + 2 * per] = jnp.concatenate(two, axis=0).astype(BF16)
    store_g = weights(0, dwg, dwg_hbm, store_sem.at[0])
    reduce_first(ng - 1)
    store_u = weights(1, dwu, dwu_hbm, store_sem.at[1])

    for j in range(n):
        pltpu.make_async_copy(sums.at[0], part2.at[j], s2_recv.at[j]).wait()
    total = part2[0].astype(F32)
    for j in range(1, n):
        total += part2[j].astype(F32)
    out_ref[...] = total.astype(BF16)
    store_g.wait()
    store_u.wait()
    for copy in pending:
        copy.wait_send()
    for slot in range(n):
        reduce_sent(slot)


def solution(mesh):
    n = mesh.shape["gx"] // 2

    def local(tokens, gate_pre, up_pre, hidden_grad, w_gate, w_up):
        per, d = tokens.shape
        rows, ff = gate_pre.shape
        groups = groups_of(n)
        ng = len(groups)
        any_spec = pl.BlockSpec(memory_space=pl.ANY)
        dma = pltpu.SemaphoreType.DMA
        half = n // 2
        scratch = [
            pltpu.VMEM((rows, ff), BF16),
            pltpu.VMEM((rows, ff), BF16),
            pltpu.VMEM((rows, ff), BF16),
            pltpu.VMEM((d, ff), BF16),
            pltpu.VMEM((d, ff), BF16),
            pltpu.VMEM((2, n, 2, rows, ff), BF16),
            pltpu.VMEM((n, n, per, d), BF16),
            pltpu.VMEM((n * n * per, d), BF16),
            pltpu.VMEM((d, ff), BF16),
            pltpu.VMEM((d, ff), BF16),
            pltpu.VMEM((n, per, d), BF16),
            pltpu.VMEM((n, per, d), BF16),
        ]
        scratch += [pltpu.VMEM((n, hi - lo, per, d), BF16) for lo, hi in groups]
        scratch += [pltpu.VMEM((n - 1, hi - lo, per, d), BF16) for lo, hi in groups]
        scratch += [
            dma((6,)), dma((2,)),
            dma((2, half, 2)), dma((2, half, 2)),
            dma((n, 2)), dma((n, 2)),
            dma((n - 1,)), dma((n - 1,)),
            dma((2, half)), dma((2, half)),
            dma((ng, n - 1)), dma((ng, n - 1)),
            dma((n,)), dma((n,)),
        ]
        return pl.pallas_call(
            functools.partial(kernel, n, rows),
            out_shape=(
                jax.ShapeDtypeStruct((per, d), BF16),
                jax.ShapeDtypeStruct((d, ff), BF16),
                jax.ShapeDtypeStruct((d, ff), BF16),
            ),
            in_specs=[any_spec] * 6,
            out_specs=(pl.BlockSpec(memory_space=pltpu.VMEM), any_spec, any_spec),
            scratch_shapes=scratch,
            compiler_params=pltpu.CompilerParams(
                collective_id=0, has_side_effects=True,
                vmem_limit_bytes=48 * 1024 * 1024,
            ),
            cost_estimate=pl.CostEstimate(
                flops=8 * n * n * per * d * ff, bytes_accessed=8 * d * ff,
                transcendentals=rows * ff,
            ),
        )(tokens, gate_pre, up_pre, hidden_grad, w_gate, w_up)

    return jax.shard_map(
        local,
        mesh=mesh,
        in_specs=(
            P("gy", "gx"),
            P("gx", "gy"),
            P("gx", "gy"),
            P("gx", "gy"),
            P("gx", "gy"),
            P("gx", "gy"),
        ),
        out_specs=(P("gy", "gx"), P("gx", "gy"), P("gx", "gy")),
        check_vma=False,
    )
```

```python
import functools

import jax
import jax.numpy as jnp
from jax import lax
from jax.experimental import pallas as pl
from jax.experimental.pallas import tpu as pltpu
from jax.sharding import PartitionSpec as P

MESH = pl.DeviceIdType.MESH
F32 = jnp.float32
BF16 = jnp.bfloat16
VMEM_MIB = 60


ORDER = (0, 2, 6, 1, 7, 3, 5, 4)
SLOT = {delta: slot for slot, delta in enumerate(ORDER)}
GROUPS = ((0, 1), (1, 3), (3, 5), (5, 8))
N = 8


def kernel(rows, *refs):
    (
        tok_hbm, gate_hbm, up_hbm, grad_hbm, wg_hbm, wu_hbm,
        out_ref, dwg_hbm, dwu_hbm,
        gate_v, up_v, grad_v, wg, wu, gu, tok, tok2, dwg, dwu, sums, part2,
        *more,
    ) = refs
    n = N
    ng = len(GROUPS)
    parts = more[:ng]
    recvs = more[ng:2 * ng]
    (
        load_sem, store_sem, z_send, z_recv, sib_send, sib_recv,
        t1_send, t1_recv, t2_send, t2_recv, s1_send, s1_recv, s2_send, s2_recv,
        near_sem,
    ) = more[2 * ng:]
    gx = lax.axis_index("gx")
    gy = lax.axis_index("gy")
    z, c = gx // 2, gx % 2
    x, y = gy // n, gy % n

    def at_z(step):
        return (((z + step + n) % n) * 2 + c, gy)

    def at_x(step):
        return (gx, ((x + step + n) % n) * n + y)

    def at_y(step):
        return (gx, x * n + (y + step + n) % n)

    sibling = (gx + 1 - 2 * c, gy)

    def signal(sem, to):
        pl.semaphore_signal(sem, inc=1, device_id=to, device_id_type=MESH)

    def copy_of(src, dst, send, recv, to):
        return pltpu.make_async_remote_copy(
            src_ref=src, dst_ref=dst, send_sem=send, recv_sem=recv,
            device_id=to, device_id_type=MESH,
        )

    pending = []

    def remote(*args):
        copy = copy_of(*args)
        copy.start()
        pending.append(copy)

    loads = [
        pltpu.make_async_copy(src, dst, load_sem.at[i])
        for i, (src, dst) in enumerate(
            (
                (gate_hbm, gate_v), (up_hbm, up_v), (grad_hbm, grad_v),
                (tok_hbm, tok.at[x, y]), (wg_hbm, wg), (wu_hbm, wu),
            )
        )
    ]
    for load in loads:
        load.start()

    barrier = pltpu.get_barrier_semaphore()
    near = (1, -1, 2, -2)
    for step in near:
        signal(barrier, at_z(step))
    signal(barrier, sibling)
    for step in near:
        signal(barrier, at_x(step))
        signal(barrier, at_y(step))

    for load in loads[:3]:
        load.wait()
    gate = gate_v[...].astype(F32)
    up = up_v[...].astype(F32)
    grad = grad_v[...].astype(F32)
    sig = 1.0 / (1.0 + jnp.exp(-gate))
    gu[0, 0, c] = (grad * up * sig * (1.0 + gate * (1.0 - sig))).astype(BF16)
    gu[1, 0, c] = (grad * gate * sig).astype(BF16)

    pl.semaphore_wait(barrier, 13)

    def z_send_on(held, via, chunk):
        delta = (held + via) % n
        remote(
            gu.at[chunk, SLOT[held % n], c], gu.at[chunk, SLOT[delta], c],
            z_send.at[SLOT[delta], chunk], z_recv.at[SLOT[delta], chunk],
            at_z(-via),
        )

    def z_wait(delta, chunk):
        ref = gu.at[chunk, SLOT[delta % n], c]
        copy_of(
            ref, ref, z_send.at[SLOT[delta % n], chunk],
            z_recv.at[SLOT[delta % n], chunk], sibling,
        ).wait_recv()

    def sib_share(delta, chunk):
        slot = SLOT[delta % n]
        ref = gu.at[chunk, slot, c]
        remote(ref, ref, sib_send.at[slot, chunk], sib_recv.at[slot, chunk], sibling)

    def sib_wait(delta, chunk):
        slot = SLOT[delta % n]
        ref = gu.at[chunk, slot, 1 - c]
        copy_of(
            ref, ref, sib_send.at[slot, chunk], sib_recv.at[slot, chunk], sibling
        ).wait_recv()

    for chunk in range(2):
        for via in (2, -2):
            z_send_on(0, via, chunk)
    for chunk in range(2):
        sib_share(0, chunk)
    for chunk in range(2):
        for via in (1, -1):
            z_send_on(0, via, chunk)

    for step in (2, -2):
        signal(near_sem, at_x(step))
        signal(near_sem, at_y(step))
    loads[3].wait()
    pl.semaphore_wait(near_sem, 4)

    for k in (4, 3, 5, 2, 6, 1, 7):
        remote(
            tok.at[x, y], tok.at[x, y], t1_send.at[k - 1], t1_recv.at[k - 1], at_y(k)
        )

    def tok_first_wait():
        for k in range(1, n):
            ref = tok.at[x, (y + n - k) % n]
            copy_of(
                ref, ref, t1_send.at[k - 1], t1_recv.at[k - 1], sibling
            ).wait_recv()

    def tok_send_on(held, via, lo=0, hi=N):
        delta = (held + via) % n
        ref = tok.at[(x + held + n) % n, lo:hi]
        at = SLOT[delta] if (lo, hi) != (n // 2, n) else 0
        remote(ref, ref, t2_send.at[at], t2_recv.at[at], at_x(-via))

    def tok_wait(delta, lo=0, hi=N):
        ref = tok.at[(x + delta + n) % n, lo:hi]
        at = SLOT[delta % n] if (lo, hi) != (n // 2, n) else 0
        copy_of(ref, ref, t2_send.at[at], t2_recv.at[at], sibling).wait_recv()

    def tok_relay():
        for side in (2, -2):
            tok_wait(side)
            tok_send_on(side, side, *((0, n // 2) if side == 2 else (n // 2, n)))
            tok_send_on(side, side // 2)

    def multiply(index):
        lo, hi = GROUPS[index]
        block = 2 * rows
        m = (hi - lo) * block
        dims = (((1,), (1,)), ((), ()))
        total = lax.dot_general(
            gu[0, lo:hi].reshape(m, gu.shape[-1]), wg[...], dims,
            preferred_element_type=F32,
        )
        total += lax.dot_general(
            gu[1, lo:hi].reshape(m, gu.shape[-1]), wu[...], dims,
            preferred_element_type=F32,
        )
        for i in range(hi - lo):
            parts[index][:, i] = (
                total[i * block:(i + 1) * block]
                .reshape(n, block // n, total.shape[-1]).astype(BF16)
            )
        for k in (4, 3, 5, 2, 6, 1, 7):
            remote(
                parts[index].at[(y + k) % n], recvs[index].at[k - 1],
                s1_send.at[index, k - 1], s1_recv.at[index, k - 1], at_y(k),
            )

    def reduce_first(index):
        lo, hi = GROUPS[index]
        for k in range(1, n):
            ref = recvs[index].at[k - 1]
            copy_of(
                ref, ref, s1_send.at[index, k - 1], s1_recv.at[index, k - 1], sibling
            ).wait_recv()
        total = parts[index][y].astype(F32)
        for k in range(1, n):
            total += recvs[index][k - 1].astype(F32)
        sums[lo:hi] = total.astype(BF16)
        for slot in range(lo, hi):
            owner = (z + ORDER[slot]) % n

            @pl.when(owner == x)
            def _():
                pltpu.make_async_copy(
                    sums.at[slot], part2.at[x], s2_recv.at[x]
                ).start()

            @pl.when(owner != x)
            def _():
                copy_of(
                    sums.at[slot], part2.at[x], s2_send.at[slot], s2_recv.at[x],
                    (gx, owner * n + y),
                ).start()

    def weights(chunk, result, to, sem):
        right = gu[chunk].reshape(n * 2 * rows, gu.shape[-1])
        result[...] = lax.dot_general(
            tok2[...], right, (((0,), (0,)), ((), ())), preferred_element_type=F32
        ).astype(BF16)
        store = pltpu.make_async_copy(result, to, sem)
        store.start()
        return store

    loads[4].wait()
    loads[5].wait()
    for chunk in range(2):
        sib_wait(0, chunk)
    multiply(0)

    for chunk in range(2):
        for side in (2, -2):
            z_wait(side, chunk)
            if (chunk == 0) == (side == 2):
                z_send_on(side, side, chunk)
            z_send_on(side, side // 2, chunk)
            sib_share(side, chunk)
    for chunk in range(2):
        for side in (2, -2):
            sib_wait(side, chunk)
    multiply(1)

    tok_first_wait()
    for via in (2, -2, 1, -1):
        tok_send_on(0, via)

    for chunk in range(2):
        for side in (1, -1):
            z_wait(side, chunk)
            sib_share(side, chunk)
    for chunk in range(2):
        for side in (1, -1):
            sib_wait(side, chunk)
    multiply(2)

    reduce_first(0)

    for chunk in range(2):
        for side in (3, -3):
            z_wait(side, chunk)
            sib_share(side, chunk)
        z_wait(4, chunk)
        sib_share(4, chunk)
    tok_relay()
    for chunk in range(2):
        for side in (3, -3, 4):
            sib_wait(side, chunk)
    multiply(3)
    reduce_first(1)
    reduce_first(2)

    for side in (1, -1, 3, -3):
        tok_wait(side)
    tok_wait(4, 0, n // 2)
    tok_wait(4, n // 2, n)

    per = tok.shape[2]
    for slot in range(n):
        block = (z + ORDER[slot]) % n
        for pair in range(n // 2):
            two = tok[block, 2 * pair:2 * pair + 2].astype(F32)
            start = (slot * n + 2 * pair) * per
            tok2[start:start + 2 * per] = (
                two.reshape(2 * per, tok.shape[-1]).astype(BF16)
            )
    store_g = weights(0, dwg, dwg_hbm, store_sem.at[0])
    store_u = weights(1, dwu, dwu_hbm, store_sem.at[1])
    reduce_first(3)

    for copy in pending:
        copy.wait_send()
    store_g.wait()
    store_u.wait()
    for j in range(n):
        pltpu.make_async_copy(sums.at[0], part2.at[j], s2_recv.at[j]).wait()
    total = part2[0].astype(F32)
    for j in range(1, n):
        total += part2[j].astype(F32)
    out_ref[...] = total.astype(BF16)
    for slot in range(n):
        @pl.when((z + ORDER[slot]) % n != x)
        def _():
            copy_of(
                sums.at[slot], part2.at[0], s2_send.at[slot], s2_recv.at[0], sibling
            ).wait_send()


def solution(mesh):
    def local(tokens, gate_pre, up_pre, hidden_grad, w_gate, w_up):
        per, d = tokens.shape
        rows, ff = gate_pre.shape
        n = N
        ng = len(GROUPS)
        hbm = pl.BlockSpec(memory_space=pltpu.HBM)
        anywhere = pl.BlockSpec(memory_space=pl.ANY)
        dma = pltpu.SemaphoreType.DMA
        scratch = [
            pltpu.VMEM((rows, ff), BF16),
            pltpu.VMEM((rows, ff), BF16),
            pltpu.VMEM((rows, ff), BF16),
            pltpu.VMEM((d, ff), BF16),
            pltpu.VMEM((d, ff), BF16),
            pltpu.VMEM((2, n, 2, rows, ff), BF16),
            pltpu.VMEM((n, n, per, d), BF16),
            pltpu.VMEM((n * n * per, d), BF16),
            pltpu.VMEM((d, ff), BF16),
            pltpu.VMEM((d, ff), BF16),
            pltpu.VMEM((n, per, d), BF16),
            pltpu.VMEM((n, per, d), BF16),
        ]
        scratch += [pltpu.VMEM((n, hi - lo, per, d), BF16) for lo, hi in GROUPS]
        scratch += [pltpu.VMEM((n - 1, hi - lo, per, d), BF16) for lo, hi in GROUPS]
        scratch += [
            dma((6,)), dma((2,)),
            dma((n, 2)), dma((n, 2)),
            dma((n, 2)), dma((n, 2)),
            dma((n - 1,)), dma((n - 1,)),
            dma((n,)), dma((n,)),
            dma((ng, n - 1)), dma((ng, n - 1)),
            dma((n,)), dma((n,)),
            pltpu.SemaphoreType.REGULAR,
        ]
        return pl.pallas_call(
            functools.partial(kernel, rows),
            out_shape=(
                jax.ShapeDtypeStruct((per, d), BF16),
                jax.ShapeDtypeStruct((d, ff), BF16),
                jax.ShapeDtypeStruct((d, ff), BF16),
            ),
            in_specs=[hbm] * 6,
            out_specs=(pl.BlockSpec(memory_space=pltpu.VMEM), anywhere, anywhere),
            scratch_shapes=scratch,
            compiler_params=pltpu.CompilerParams(
                collective_id=0, has_side_effects=True,
                vmem_limit_bytes=VMEM_MIB * 1024 * 1024,
            ),
            cost_estimate=pl.CostEstimate(
                flops=8 * n * n * per * d * ff, bytes_accessed=8 * d * ff,
                transcendentals=rows * ff,
            ),
        )(tokens, gate_pre, up_pre, hidden_grad, w_gate, w_up)

    return jax.shard_map(
        local,
        mesh=mesh,
        in_specs=(
            P("gy", "gx"),
            P("gx", "gy"),
            P("gx", "gy"),
            P("gx", "gy"),
            P("gx", "gy"),
            P("gx", "gy"),
        ),
        out_specs=(P("gy", "gx"), P("gx", "gy"), P("gx", "gy")),
        check_vma=False,
    )
```

```python
import functools

import jax
import jax.numpy as jnp
from jax import lax
from jax.experimental import pallas as pl
from jax.experimental.pallas import tpu as pltpu
from jax.sharding import PartitionSpec as P

MESH = pl.DeviceIdType.MESH
F32 = jnp.float32
BF16 = jnp.bfloat16
VMEM_MIB = 60


GROUPS = ((0, 3), (3, 5), (5, 7), (7, 8))
AHEAD = 3
N = 8


def kernel(rows, *refs):
    (
        tok_hbm, gate_hbm, up_hbm, grad_hbm, wg_hbm, wu_hbm,
        out_ref, dwg_hbm, dwu_hbm,
        gate_v, up_v, grad_v, wg, wu, gu, tok, tok2, dwg, dwu, sums, part2,
        *more,
    ) = refs
    n = N
    ng = len(GROUPS)
    parts = more[:ng]
    recvs = more[ng:2 * ng]
    (
        load_sem, store_sem, z_send, z_recv, sib_send, sib_recv,
        t1_send, t1_recv, t2_send, t2_recv, s1_send, s1_recv, s2_send, s2_recv,
        near_sem, up_sem,
    ) = more[2 * ng:]
    gx = lax.axis_index("gx")
    gy = lax.axis_index("gy")
    z, c = gx // 2, gx % 2
    x, y = gy // n, gy % n

    def at_z(chip):
        return (chip * 2 + c, gy)

    def at_x(step):
        return (gx, ((x + step + n) % n) * n + y)

    def at_y(step):
        return (gx, x * n + (y + step + n) % n)

    sibling = (gx + 1 - 2 * c, gy)

    def signal(sem, to):
        pl.semaphore_signal(sem, inc=1, device_id=to, device_id_type=MESH)

    def copy_of(src, dst, send, recv, to):
        return pltpu.make_async_remote_copy(
            src_ref=src, dst_ref=dst, send_sem=send, recv_sem=recv,
            device_id=to, device_id_type=MESH,
        )

    pending = []

    def remote(*args):
        copy = copy_of(*args)
        copy.start()
        pending.append(copy)

    loads = [
        pltpu.make_async_copy(src, dst, load_sem.at[i])
        for i, (src, dst) in enumerate(
            (
                (gate_hbm, gate_v), (up_hbm, up_v), (grad_hbm, grad_v),
                (tok_hbm, tok.at[x, y]), (wg_hbm, wg), (wu_hbm, wu),
            )
        )
    ]
    for load in loads:
        load.start()

    barrier = pltpu.get_barrier_semaphore()
    near = (1, -1, 2, -2)
    for chip in range(1, n):
        @pl.when(chip > z)
        def _():
            signal(barrier, at_z(chip))
    signal(barrier, sibling)
    for step in near:
        signal(barrier, at_x(step))
        signal(barrier, at_y(step))

    for load in loads[:3]:
        load.wait()
    gate = gate_v[...].astype(F32)
    up = up_v[...].astype(F32)
    grad = grad_v[...].astype(F32)
    sig = 1.0 / (1.0 + jnp.exp(-gate))
    gu[0, z, c] = (grad * up * sig * (1.0 + gate * (1.0 - sig))).astype(BF16)
    gu[1, z, c] = (grad * gate * sig).astype(BF16)

    pl.semaphore_wait(barrier, z + 9)

    def z_copy(chip):
        own = gu.at[:, z, c]
        return copy_of(own, own, z_send.at[chip], z_recv.at[z], at_z(chip))

    def z_arrive(chip):
        ref = gu.at[:, chip, c]
        copy_of(ref, ref, z_send.at[chip], z_recv.at[chip], sibling).wait_recv()

    def share(chip, half):
        ref = gu.at[:, chip, half]
        return copy_of(ref, ref, sib_send.at[chip], sib_recv.at[chip], sibling)

    share(z, c).start()
    for chip in range(n - 1):
        @pl.when(chip < z)
        def _():
            signal(up_sem.at[z], at_z(chip))
            z_copy(chip).start()

    def send_up(chip):
        pl.semaphore_wait(up_sem.at[chip], 1)
        z_copy(chip).start()

    for step in (2, -2):
        signal(near_sem, at_x(step))
        signal(near_sem, at_y(step))
    loads[3].wait()
    pl.semaphore_wait(near_sem, 4)

    for k in (4, 3, 5, 2, 6, 1, 7):
        remote(
            tok.at[x, y], tok.at[x, y], t1_send.at[k - 1], t1_recv.at[k - 1], at_y(k)
        )

    def tok_first_wait():
        for k in range(1, n):
            ref = tok.at[x, (y + n - k) % n]
            copy_of(
                ref, ref, t1_send.at[k - 1], t1_recv.at[k - 1], sibling
            ).wait_recv()

    def tok_send_on(held, via, lo=0, hi=N):
        delta = (held + via) % n
        ref = tok.at[(x + held + n) % n, lo:hi]
        at = delta if (lo, hi) != (n // 2, n) else 0
        remote(ref, ref, t2_send.at[at], t2_recv.at[at], at_x(-via))

    def tok_wait(delta, lo=0, hi=N):
        ref = tok.at[(x + delta + n) % n, lo:hi]
        at = delta % n if (lo, hi) != (n // 2, n) else 0
        copy_of(ref, ref, t2_send.at[at], t2_recv.at[at], sibling).wait_recv()

    def tok_relay():
        for side in (2, -2):
            tok_wait(side)
            tok_send_on(side, side, *((0, n // 2) if side == 2 else (n // 2, n)))
            tok_send_on(side, side // 2)

    def multiply(index):
        lo, hi = GROUPS[index]
        block = 2 * rows
        m = (hi - lo) * block
        dims = (((1,), (1,)), ((), ()))
        total = lax.dot_general(
            gu[0, lo:hi].reshape(m, gu.shape[-1]), wg[...], dims,
            preferred_element_type=F32,
        )
        total += lax.dot_general(
            gu[1, lo:hi].reshape(m, gu.shape[-1]), wu[...], dims,
            preferred_element_type=F32,
        )
        for i in range(hi - lo):
            parts[index][:, i] = (
                total[i * block:(i + 1) * block]
                .reshape(n, block // n, total.shape[-1]).astype(BF16)
            )
        for k in (4, 3, 5, 2, 6, 1, 7):
            remote(
                parts[index].at[(y + k) % n], recvs[index].at[k - 1],
                s1_send.at[index, k - 1], s1_recv.at[index, k - 1], at_y(k),
            )

    def reduce_first(index):
        lo, hi = GROUPS[index]
        for k in range(1, n):
            ref = recvs[index].at[k - 1]
            copy_of(
                ref, ref, s1_send.at[index, k - 1], s1_recv.at[index, k - 1], sibling
            ).wait_recv()
        total = parts[index][y].astype(F32)
        for k in range(1, n):
            total += recvs[index][k - 1].astype(F32)
        sums[lo:hi] = total.astype(BF16)
        for chip in range(lo, hi):
            @pl.when(x == chip)
            def _():
                pltpu.make_async_copy(
                    sums.at[chip], part2.at[x], s2_recv.at[x]
                ).start()

            @pl.when(x != chip)
            def _():
                copy_of(
                    sums.at[chip], part2.at[x], s2_send.at[chip], s2_recv.at[x],
                    (gx, chip * n + y),
                ).start()

    def weights(chunk, result, to, sem):
        right = gu[chunk].reshape(n * 2 * rows, gu.shape[-1])
        result[...] = lax.dot_general(
            tok2[...], right, (((0,), (0,)), ((), ())), preferred_element_type=F32
        ).astype(BF16)
        store = pltpu.make_async_copy(result, to, sem)
        store.start()
        return store

    loads[4].wait()
    loads[5].wait()
    for chip in range(1, n):
        @pl.when((chip > z) & (chip <= z + AHEAD))
        def _():
            send_up(chip)

    for index, (lo, hi) in enumerate(GROUPS):
        for chip in range(lo, hi):
            if AHEAD < chip + AHEAD < n:
                @pl.when(chip > z)
                def _():
                    send_up(chip + AHEAD)

            @pl.when(chip != z)
            def _():
                z_arrive(chip)
                share(chip, c).start()
        for chip in range(lo, hi):
            share(chip, 1 - c).wait_recv()
        multiply(index)
        if index == 0:
            tok_first_wait()
            for via in (2, -2, 1, -1):
                tok_send_on(0, via)
    tok_relay()
    for index in range(ng - 1):
        reduce_first(index)

    for side in (1, -1, 3, -3):
        tok_wait(side)
    tok_wait(4, 0, n // 2)
    tok_wait(4, n // 2, n)

    per = tok.shape[2]
    for chip in range(n):
        for pair in range(n // 2):
            two = tok[chip, 2 * pair:2 * pair + 2].astype(F32)
            start = (chip * n + 2 * pair) * per
            tok2[start:start + 2 * per] = (
                two.reshape(2 * per, tok.shape[-1]).astype(BF16)
            )
    store_g = weights(0, dwg, dwg_hbm, store_sem.at[0])
    store_u = weights(1, dwu, dwu_hbm, store_sem.at[1])
    reduce_first(ng - 1)

    for copy in pending:
        copy.wait_send()
    store_g.wait()
    store_u.wait()
    for j in range(n):
        pltpu.make_async_copy(sums.at[0], part2.at[j], s2_recv.at[j]).wait()
    total = part2[0].astype(F32)
    for j in range(1, n):
        total += part2[j].astype(F32)
    out_ref[...] = total.astype(BF16)
    for chip in range(n):
        share(chip, c).wait_send()

        @pl.when(chip != z)
        def _():
            z_copy(chip).wait_send()

        @pl.when(chip != x)
        def _():
            copy_of(
                sums.at[chip], part2.at[0], s2_send.at[chip], s2_recv.at[0], sibling
            ).wait_send()


def solution(mesh):
    def local(tokens, gate_pre, up_pre, hidden_grad, w_gate, w_up):
        per, d = tokens.shape
        rows, ff = gate_pre.shape
        n = N
        ng = len(GROUPS)
        hbm = pl.BlockSpec(memory_space=pltpu.HBM)
        anywhere = pl.BlockSpec(memory_space=pl.ANY)
        dma = pltpu.SemaphoreType.DMA
        scratch = [
            pltpu.VMEM((rows, ff), BF16),
            pltpu.VMEM((rows, ff), BF16),
            pltpu.VMEM((rows, ff), BF16),
            pltpu.VMEM((d, ff), BF16),
            pltpu.VMEM((d, ff), BF16),
            pltpu.VMEM((2, n, 2, rows, ff), BF16),
            pltpu.VMEM((n, n, per, d), BF16),
            pltpu.VMEM((n * n * per, d), BF16),
            pltpu.VMEM((d, ff), BF16),
            pltpu.VMEM((d, ff), BF16),
            pltpu.VMEM((n, per, d), BF16),
            pltpu.VMEM((n, per, d), BF16),
        ]
        scratch += [pltpu.VMEM((n, hi - lo, per, d), BF16) for lo, hi in GROUPS]
        scratch += [pltpu.VMEM((n - 1, hi - lo, per, d), BF16) for lo, hi in GROUPS]
        scratch += [
            dma((6,)), dma((2,)),
            dma((n,)), dma((n,)),
            dma((n,)), dma((n,)),
            dma((n - 1,)), dma((n - 1,)),
            dma((n,)), dma((n,)),
            dma((ng, n - 1)), dma((ng, n - 1)),
            dma((n,)), dma((n,)),
            pltpu.SemaphoreType.REGULAR, pltpu.SemaphoreType.REGULAR((n,)),
        ]
        return pl.pallas_call(
            functools.partial(kernel, rows),
            out_shape=(
                jax.ShapeDtypeStruct((per, d), BF16),
                jax.ShapeDtypeStruct((d, ff), BF16),
                jax.ShapeDtypeStruct((d, ff), BF16),
            ),
            in_specs=[hbm] * 6,
            out_specs=(pl.BlockSpec(memory_space=pltpu.VMEM), anywhere, anywhere),
            scratch_shapes=scratch,
            compiler_params=pltpu.CompilerParams(
                collective_id=0, has_side_effects=True,
                vmem_limit_bytes=VMEM_MIB * 1024 * 1024,
            ),
            cost_estimate=pl.CostEstimate(
                flops=8 * n * n * per * d * ff, bytes_accessed=8 * d * ff,
                transcendentals=rows * ff,
            ),
        )(tokens, gate_pre, up_pre, hidden_grad, w_gate, w_up)

    return jax.shard_map(
        local,
        mesh=mesh,
        in_specs=(
            P("gy", "gx"),
            P("gx", "gy"),
            P("gx", "gy"),
            P("gx", "gy"),
            P("gx", "gy"),
            P("gx", "gy"),
        ),
        out_specs=(P("gy", "gx"), P("gx", "gy"), P("gx", "gy")),
        check_vma=False,
    )
```

```python
import functools

import jax
import jax.numpy as jnp
from jax import lax
from jax.experimental import pallas as pl
from jax.experimental.pallas import tpu as pltpu
from jax.sharding import PartitionSpec as P

MESH = pl.DeviceIdType.MESH
F32 = jnp.float32
BF16 = jnp.bfloat16
VMEM_MIB = 60


GROUPS = ((0, 3), (3, 5), (5, 7), (7, 8))
AHEAD = 3
N = 8


def kernel(rows, *refs):
    (
        tok_hbm, gate_hbm, up_hbm, grad_hbm, wg_hbm, wu_hbm,
        out_ref, dwg_hbm, dwu_hbm,
        gate_v, up_v, grad_v, wg, wu, gu, tok, tok2, dwg, dwu, sums, part2,
        *more,
    ) = refs
    n = N
    ng = len(GROUPS)
    parts = more[:ng]
    recvs = more[ng:2 * ng]
    (
        load_sem, store_sem, z_send, z_recv, sib_send, sib_recv,
        t1_send, t1_recv, t2_send, t2_recv, s1_send, s1_recv, s2_send, s2_recv,
        near_sem, up_sem,
    ) = more[2 * ng:]
    gx = lax.axis_index("gx")
    gy = lax.axis_index("gy")
    z, c = gx // 2, gx % 2
    x, y = gy // n, gy % n

    def at_z(chip):
        return (chip * 2 + c, gy)

    def at_x(step):
        return (gx, ((x + step + n) % n) * n + y)

    def at_y(step):
        return (gx, x * n + (y + step + n) % n)

    sibling = (gx + 1 - 2 * c, gy)

    def signal(sem, to):
        pl.semaphore_signal(sem, inc=1, device_id=to, device_id_type=MESH)

    def copy_of(src, dst, send, recv, to):
        return pltpu.make_async_remote_copy(
            src_ref=src, dst_ref=dst, send_sem=send, recv_sem=recv,
            device_id=to, device_id_type=MESH,
        )

    pending = []

    def remote(*args):
        copy = copy_of(*args)
        copy.start()
        pending.append(copy)

    loads = [
        pltpu.make_async_copy(src, dst, load_sem.at[i])
        for i, (src, dst) in enumerate(
            (
                (gate_hbm, gate_v), (up_hbm, up_v), (grad_hbm, grad_v),
                (tok_hbm, tok.at[x, y]), (wg_hbm, wg), (wu_hbm, wu),
            )
        )
    ]
    for load in loads:
        load.start()

    barrier = pltpu.get_barrier_semaphore()
    near = (1, -1, 2, -2)
    for chip in range(1, n):
        @pl.when(chip > z)
        def _():
            signal(barrier, at_z(chip))
    signal(barrier, sibling)
    for step in near:
        signal(barrier, at_x(step))
        signal(barrier, at_y(step))

    for load in loads[:3]:
        load.wait()
    gate = gate_v[...].astype(F32)
    up = up_v[...].astype(F32)
    grad = grad_v[...].astype(F32)
    sig = 1.0 / (1.0 + jnp.exp(-gate))
    gu[0, z, c] = (grad * up * sig * (1.0 + gate * (1.0 - sig))).astype(BF16)
    gu[1, z, c] = (grad * gate * sig).astype(BF16)

    pl.semaphore_wait(barrier, z + 9)

    def z_copy(chip):
        own = gu.at[:, z, c]
        return copy_of(own, own, z_send.at[chip], z_recv.at[z], at_z(chip))

    def z_arrive(chip):
        ref = gu.at[:, chip, c]
        copy_of(ref, ref, z_send.at[chip], z_recv.at[chip], sibling).wait_recv()

    def share(chip, half):
        ref = gu.at[:, chip, half]
        return copy_of(ref, ref, sib_send.at[chip], sib_recv.at[chip], sibling)

    share(z, c).start()
    for chip in range(n - 1):
        @pl.when(chip < z)
        def _():
            signal(up_sem.at[z], at_z(chip))
            z_copy(chip).start()

    def send_up(chip):
        pl.semaphore_wait(up_sem.at[chip], 1)
        z_copy(chip).start()

    for step in (2, -2):
        signal(near_sem, at_x(step))
        signal(near_sem, at_y(step))
    loads[3].wait()
    pl.semaphore_wait(near_sem, 4)

    for k in (4, 3, 5, 2, 6, 1, 7):
        remote(
            tok.at[x, y], tok.at[x, y], t1_send.at[k - 1], t1_recv.at[k - 1], at_y(k)
        )

    def tok_first_wait():
        for k in range(1, n):
            ref = tok.at[x, (y + n - k) % n]
            copy_of(
                ref, ref, t1_send.at[k - 1], t1_recv.at[k - 1], sibling
            ).wait_recv()

    def tok_send_on(held, via, lo=0, hi=N):
        delta = (held + via) % n
        ref = tok.at[(x + held + n) % n, lo:hi]
        at = delta if (lo, hi) != (n // 2, n) else 0
        remote(ref, ref, t2_send.at[at], t2_recv.at[at], at_x(-via))

    def tok_wait(delta, lo=0, hi=N):
        ref = tok.at[(x + delta + n) % n, lo:hi]
        at = delta % n if (lo, hi) != (n // 2, n) else 0
        copy_of(ref, ref, t2_send.at[at], t2_recv.at[at], sibling).wait_recv()

    def tok_relay():
        for side in (2, -2):
            tok_wait(side)
            tok_send_on(side, side, *((0, n // 2) if side == 2 else (n // 2, n)))
            tok_send_on(side, side // 2)

    def multiply(index):
        lo, hi = GROUPS[index]
        block = 2 * rows
        m = (hi - lo) * block
        dims = (((1,), (1,)), ((), ()))
        total = lax.dot_general(
            gu[0, lo:hi].reshape(m, gu.shape[-1]), wg[...], dims,
            preferred_element_type=F32,
        )
        total += lax.dot_general(
            gu[1, lo:hi].reshape(m, gu.shape[-1]), wu[...], dims,
            preferred_element_type=F32,
        )
        for i in range(hi - lo):
            parts[index][:, i] = (
                total[i * block:(i + 1) * block]
                .reshape(n, block // n, total.shape[-1]).astype(BF16)
            )
        for k in (4, 3, 5, 2, 6, 1, 7):
            remote(
                parts[index].at[(y + k) % n], recvs[index].at[k - 1],
                s1_send.at[index, k - 1], s1_recv.at[index, k - 1], at_y(k),
            )

    def reduce_first(index):
        lo, hi = GROUPS[index]
        for k in range(1, n):
            ref = recvs[index].at[k - 1]
            copy_of(
                ref, ref, s1_send.at[index, k - 1], s1_recv.at[index, k - 1], sibling
            ).wait_recv()
        total = parts[index][y].astype(F32)
        for k in range(1, n):
            total += recvs[index][k - 1].astype(F32)
        sums[lo:hi] = total.astype(BF16)
        for chip in range(lo, hi):
            @pl.when(x == chip)
            def _():
                pltpu.make_async_copy(
                    sums.at[chip], part2.at[x], s2_recv.at[x]
                ).start()

            @pl.when(x != chip)
            def _():
                copy_of(
                    sums.at[chip], part2.at[x], s2_send.at[chip], s2_recv.at[x],
                    (gx, chip * n + y),
                ).start()

    def weights(chunk, result, to, sem):
        right = gu[chunk].reshape(n * 2 * rows, gu.shape[-1])
        result[...] = lax.dot_general(
            tok2[...], right, (((0,), (0,)), ((), ())), preferred_element_type=F32
        ).astype(BF16)
        store = pltpu.make_async_copy(result, to, sem)
        store.start()
        return store

    loads[4].wait()
    loads[5].wait()
    for chip in range(1, n):
        @pl.when((chip > z) & (chip <= z + AHEAD))
        def _():
            send_up(chip)

    tok_first_wait()
    for via in (2, -2, 1, -1):
        tok_send_on(0, via)

    for index, (lo, hi) in enumerate(GROUPS):
        for chip in range(lo, hi):
            if AHEAD < chip + AHEAD < n:
                @pl.when(chip > z)
                def _():
                    send_up(chip + AHEAD)

            @pl.when(chip != z)
            def _():
                z_arrive(chip)
                share(chip, c).start()
        for chip in range(lo, hi):
            share(chip, 1 - c).wait_recv()
        multiply(index)
        if index == 0:
            tok_relay()
    for index in range(ng - 1):
        reduce_first(index)

    for side in (1, -1, 3, -3):
        tok_wait(side)
    tok_wait(4, 0, n // 2)
    tok_wait(4, n // 2, n)

    per = tok.shape[2]
    for chip in range(n):
        for pair in range(n // 2):
            two = tok[chip, 2 * pair:2 * pair + 2].astype(F32)
            start = (chip * n + 2 * pair) * per
            tok2[start:start + 2 * per] = (
                two.reshape(2 * per, tok.shape[-1]).astype(BF16)
            )
    store_g = weights(0, dwg, dwg_hbm, store_sem.at[0])
    store_u = weights(1, dwu, dwu_hbm, store_sem.at[1])
    reduce_first(ng - 1)

    for copy in pending:
        copy.wait_send()
    store_g.wait()
    store_u.wait()
    for j in range(n):
        pltpu.make_async_copy(sums.at[0], part2.at[j], s2_recv.at[j]).wait()
    total = part2[0].astype(F32)
    for j in range(1, n):
        total += part2[j].astype(F32)
    out_ref[...] = total.astype(BF16)
    for chip in range(n):
        share(chip, c).wait_send()

        @pl.when(chip != z)
        def _():
            z_copy(chip).wait_send()

        @pl.when(chip != x)
        def _():
            copy_of(
                sums.at[chip], part2.at[0], s2_send.at[chip], s2_recv.at[0], sibling
            ).wait_send()


def solution(mesh):
    def local(tokens, gate_pre, up_pre, hidden_grad, w_gate, w_up):
        per, d = tokens.shape
        rows, ff = gate_pre.shape
        n = N
        ng = len(GROUPS)
        hbm = pl.BlockSpec(memory_space=pltpu.HBM)
        anywhere = pl.BlockSpec(memory_space=pl.ANY)
        dma = pltpu.SemaphoreType.DMA
        scratch = [
            pltpu.VMEM((rows, ff), BF16),
            pltpu.VMEM((rows, ff), BF16),
            pltpu.VMEM((rows, ff), BF16),
            pltpu.VMEM((d, ff), BF16),
            pltpu.VMEM((d, ff), BF16),
            pltpu.VMEM((2, n, 2, rows, ff), BF16),
            pltpu.VMEM((n, n, per, d), BF16),
            pltpu.VMEM((n * n * per, d), BF16),
            pltpu.VMEM((d, ff), BF16),
            pltpu.VMEM((d, ff), BF16),
            pltpu.VMEM((n, per, d), BF16),
            pltpu.VMEM((n, per, d), BF16),
        ]
        scratch += [pltpu.VMEM((n, hi - lo, per, d), BF16) for lo, hi in GROUPS]
        scratch += [pltpu.VMEM((n - 1, hi - lo, per, d), BF16) for lo, hi in GROUPS]
        scratch += [
            dma((6,)), dma((2,)),
            dma((n,)), dma((n,)),
            dma((n,)), dma((n,)),
            dma((n - 1,)), dma((n - 1,)),
            dma((n,)), dma((n,)),
            dma((ng, n - 1)), dma((ng, n - 1)),
            dma((n,)), dma((n,)),
            pltpu.SemaphoreType.REGULAR, pltpu.SemaphoreType.REGULAR((n,)),
        ]
        return pl.pallas_call(
            functools.partial(kernel, rows),
            out_shape=(
                jax.ShapeDtypeStruct((per, d), BF16),
                jax.ShapeDtypeStruct((d, ff), BF16),
                jax.ShapeDtypeStruct((d, ff), BF16),
            ),
            in_specs=[hbm] * 6,
            out_specs=(pl.BlockSpec(memory_space=pltpu.VMEM), anywhere, anywhere),
            scratch_shapes=scratch,
            compiler_params=pltpu.CompilerParams(
                collective_id=0, has_side_effects=True,
                vmem_limit_bytes=VMEM_MIB * 1024 * 1024,
            ),
            cost_estimate=pl.CostEstimate(
                flops=8 * n * n * per * d * ff, bytes_accessed=8 * d * ff,
                transcendentals=rows * ff,
            ),
        )(tokens, gate_pre, up_pre, hidden_grad, w_gate, w_up)

    return jax.shard_map(
        local,
        mesh=mesh,
        in_specs=(
            P("gy", "gx"),
            P("gx", "gy"),
            P("gx", "gy"),
            P("gx", "gy"),
            P("gx", "gy"),
            P("gx", "gy"),
        ),
        out_specs=(P("gy", "gx"), P("gx", "gy"), P("gx", "gy")),
        check_vma=False,
    )
```
